32 devices in a mesh: grp: 2 (over x), dom: 16 (over z, y, core).
Axes of the slice: x: 2, y: 2, z: 4, core: 2. Of those that a mesh axis runs over, the one named last changes fastest.
Arguments:
- node_latent: bfloat16 [16384, 128], P(('grp', 'dom')), parts along dimension 0, may hold values from -6 to 6
- edge_latent: bfloat16 [98304, 128], P(('grp', 'dom')), parts along dimension 0, may hold values from -6 to 6
- coarse_edge_latent: bfloat16 [49152, 128], P(('grp', 'dom')), parts along dimension 0, may hold values from -6 to 6
- edge_sender: int32 [98304], P(('grp', 'dom')), parts along dimension 0, may hold values from 0 to 671, as said below
- edge_receiver: int32 [98304], P(('grp', 'dom')), parts along dimension 0, may hold values from -1 to 511, as said below
- halo_list: int32 [5120], P(('grp', 'dom')), parts along dimension 0, may hold values from 0 to 511, as said below
- parent: int32 [16384], P(('grp', 'dom')), parts along dimension 0, may hold values from 0 to 511, as said below
- coarse_sender: int32 [49152], P(('grp', 'dom')), parts along dimension 0, may hold values from 0 to 1535, as said below
- coarse_receiver: int32 [49152], P(('grp', 'dom')), parts along dimension 0, may hold values from 0 to 511
- first_edge_in: bfloat16 [384, 128], replicated, may hold values from -0.3125 to 0.3125
- first_edge_out: bfloat16 [128, 128], replicated, may hold values from -0.5 to 0.5
- first_node_in: bfloat16 [256, 128], replicated, may hold values from -0.375 to 0.375
- first_node_out: bfloat16 [128, 128], replicated, may hold values from -0.5 to 0.5
- coarse_edge_in: bfloat16 [384, 128], replicated, may hold values from -0.3125 to 0.3125
- coarse_edge_out: bfloat16 [128, 128], replicated, may hold values from -0.5 to 0.5
- coarse_node_in: bfloat16 [256, 128], replicated, may hold values from -0.375 to 0.375
- coarse_node_out: bfloat16 [128, 128], replicated, may hold values from -0.5 to 0.5
- second_edge_in: bfloat16 [384, 128], replicated, may hold values from -0.3125 to 0.3125
- second_edge_out: bfloat16 [128, 128], replicated, may hold values from -0.5 to 0.5
- second_node_in: bfloat16 [256, 128], replicated, may hold values from -0.375 to 0.375
- second_node_out: bfloat16 [128, 128], replicated, may hold values from -0.5 to 0.5
Outputs:
- updated_nodes: bfloat16 [16384, 128], P(('grp', 'dom')), parts along dimension 0
The draws below stay inside these ranges and needn't reach their ends.
There are 2 independent parts, one for each index of `grp`. The reference program is written for one: setup_inputs(seed, part) draws one part's arguments, and reference() takes and returns one part's arrays. A program takes and returns all parts, laid end to end along the dimension named above; an argument that names none is the same for every part. Nothing has to cross between parts.
Inputs may be any that keep to these rules, and one draw needn't show every extreme that they name: `edge_receiver`: each partition's 3072 rows hold its live edges first and -1 in every later row; every partition has at least half its rows live, and some partition has no -1. `edge_sender`: indexes the partition's halo table of 672 rows. `halo_list`: Partition-local node numbers. Every coarse node of a block is the parent of at least one fine node of the block's four partitions. `coarse_sender`: indexes the block's coarse table of 1536 rows.
All inputs are finite; a program needn't handle non-finite values.
Results may differ from the reference program's by a relative error of at most 0.012.
Values may be sent and summed in bfloat16 or wider, within the bound.
A program may use at most 64 MiB of HBM per device.

```python
import jax
import jax.numpy as jnp
from jax import lax

LATENT = 128
NODE_DEV = 512
EDGE_DEV = 3072
CEDGE_DEV = 1536
SLOT = 32
PARTITIONS = 16
BLOCKS = 4
NODES = 8192
EDGES = 49152
CEDGES = 24576
SENDS = 2560


def draw_edge_receiver(key, part):
    key = jax.random.fold_in(key, 11)
    first_key, second_key = jax.random.split(key, 2)
    row_ids = jax.random.randint(first_key, (PARTITIONS, EDGE_DEV), 0, NODE_DEV)
    row_ids = row_ids.at[:, 0].set(NODE_DEV - 1)
    live_count = EDGE_DEV - jax.random.randint(second_key, (PARTITIONS,), 0, EDGE_DEV // 2)
    live_count = live_count.at[0].set(EDGE_DEV).at[1].set(EDGE_DEV // 2)
    position = jnp.arange(EDGE_DEV)[None, :]
    row_ids = jnp.where(position < live_count[:, None], row_ids, -1)
    return row_ids.reshape(EDGES).astype(jnp.int32)


def draw_edge_sender(key, part):
    key = jax.random.fold_in(key, 12)
    first_key, second_key, third_key = jax.random.split(key, 3)
    choose = jax.random.randint(first_key, (PARTITIONS, EDGE_DEV), 0, 4)
    local_ids = jax.random.randint(second_key, (PARTITIONS, EDGE_DEV), 0, NODE_DEV)
    halo_ids = NODE_DEV + jax.random.randint(third_key, (PARTITIONS, EDGE_DEV), 0, 5 * SLOT)
    picked = jnp.where(choose < 3, local_ids, halo_ids)
    picked = picked.at[:, 0].set(NODE_DEV + 5 * SLOT - 1).at[:, 1].set(0)
    return picked.reshape(EDGES).astype(jnp.int32)


def draw_halo_list(key, part):
    key = jax.random.fold_in(key, 13)
    picked = jax.random.randint(key, (SENDS,), 0, NODE_DEV)
    picked = picked.at[0].set(NODE_DEV - 1).at[1].set(0)
    return picked.astype(jnp.int32)


def draw_parent(key, part):
    key = jax.random.fold_in(key, 14)
    first_key, second_key = jax.random.split(key, 2)
    parents = jax.random.randint(first_key, (BLOCKS, 4 * NODE_DEV), 0, NODE_DEV)
    block_keys = jax.random.split(second_key, BLOCKS)
    orders = jax.vmap(lambda one_key: jax.random.permutation(one_key, 4 * NODE_DEV))(block_keys)
    every_id = jnp.arange(NODE_DEV, dtype=jnp.int32)
    parents = jax.vmap(lambda block_parents, order: block_parents.at[order[:NODE_DEV]].set(every_id))(parents, orders)
    return parents.reshape(NODES).astype(jnp.int32)


def draw_coarse_sender(key, part):
    key = jax.random.fold_in(key, 15)
    first_key, second_key = jax.random.split(key, 2)
    choose = jax.random.randint(first_key, (CEDGES,), 0, 4)
    region = jnp.where(choose < 2, 0, choose - 1)
    picked = region * NODE_DEV + jax.random.randint(second_key, (CEDGES,), 0, NODE_DEV)
    picked = picked.at[0].set(3 * NODE_DEV - 1).at[1].set(0)
    return picked.astype(jnp.int32)


def draw_coarse_receiver(key, part):
    key = jax.random.fold_in(key, 16)
    picked = jax.random.randint(key, (CEDGES,), 0, NODE_DEV)
    picked = picked.at[0].set(NODE_DEV - 1).at[1].set(0)
    return picked.astype(jnp.int32)


def level_of(rng, dims, cuts, smallest, high):
    level, own = 1.0, jax.random.fold_in(rng, 6)
    for axis_at, shards_of in cuts:
        draws = jnp.exp(jax.random.uniform(jax.random.fold_in(own, axis_at), (shards_of,), jnp.float32, smallest / len(cuts), high / len(cuts)))
        level = level * jnp.repeat(draws, dims[axis_at] // shards_of).reshape([-1 if axis == axis_at else 1 for axis in range(len(dims))])
    return level


def noise(rng, shape, scale, reach, cuts=(), held_as=jnp.bfloat16):
    drawn = jax.random.normal(rng, shape, jnp.float32) * scale
    if len(cuts) > 0:
        drawn = level_of(rng, shape, cuts, -0.22, 0.18) * drawn
    return jnp.clip(drawn, min=-reach, max=reach).astype(held_as)


def setup_inputs(seed: int = 0, part: int = 0) -> dict:
    key_of = jax.random.split(jax.random.key(seed), 22)
    part_splits = jax.random.split(jax.random.fold_in(key_of[21], part), 22)
    return {
        "node_latent": noise(part_splits[0], (NODES, LATENT), 1.0, 6.0, ((0, 16),)),
        "edge_latent": noise(part_splits[1], (EDGES, LATENT), 1.0, 6.0, ((0, 16),)),
        "coarse_edge_latent": noise(part_splits[2], (CEDGES, LATENT), 1.0, 6.0, ((0, 16),)),
        "edge_sender": draw_edge_sender(jax.random.fold_in(jax.random.fold_in(key_of[21], part), 71), part),
        "edge_receiver": draw_edge_receiver(jax.random.fold_in(jax.random.fold_in(key_of[21], part), 71), part),
        "halo_list": draw_halo_list(jax.random.fold_in(jax.random.fold_in(key_of[21], part), 71), part),
        "parent": draw_parent(jax.random.fold_in(jax.random.fold_in(key_of[21], part), 71), part),
        "coarse_sender": draw_coarse_sender(jax.random.fold_in(jax.random.fold_in(key_of[21], part), 71), part),
        "coarse_receiver": draw_coarse_receiver(jax.random.fold_in(jax.random.fold_in(key_of[21], part), 71), part),
        "first_edge_in": noise(key_of[9], (3 * LATENT, LATENT), (3 * LATENT) ** -0.5, 0.3125),
        "first_edge_out": noise(key_of[10], (LATENT, LATENT), LATENT ** -0.5, 0.5),
        "first_node_in": noise(key_of[11], (2 * LATENT, LATENT), (2 * LATENT) ** -0.5, 0.375),
        "first_node_out": noise(key_of[12], (LATENT, LATENT), LATENT ** -0.5, 0.5),
        "coarse_edge_in": noise(key_of[13], (3 * LATENT, LATENT), (3 * LATENT) ** -0.5, 0.3125),
        "coarse_edge_out": noise(key_of[14], (LATENT, LATENT), LATENT ** -0.5, 0.5),
        "coarse_node_in": noise(key_of[15], (2 * LATENT, LATENT), (2 * LATENT) ** -0.5, 0.375),
        "coarse_node_out": noise(key_of[16], (LATENT, LATENT), LATENT ** -0.5, 0.5),
        "second_edge_in": noise(key_of[17], (3 * LATENT, LATENT), (3 * LATENT) ** -0.5, 0.3125),
        "second_edge_out": noise(key_of[18], (LATENT, LATENT), LATENT ** -0.5, 0.5),
        "second_node_in": noise(key_of[19], (2 * LATENT, LATENT), (2 * LATENT) ** -0.5, 0.375),
        "second_node_out": noise(key_of[20], (LATENT, LATENT), LATENT ** -0.5, 0.5),
    }


def layer_norm(values):
    centre = lax.optimization_barrier(jnp.mean(values, axis=-1, keepdims=True))
    shifted = values - centre
    spread = lax.optimization_barrier(jnp.mean(shifted * shifted, axis=-1, keepdims=True))
    return shifted * lax.rsqrt(spread + 1e-05)

def edge_pass(node_rows, table, edge_rows, senders, receivers, weight_in, weight_out):
    node_count, row_width = node_rows.shape
    target = jnp.where(receivers < 0, node_count, receivers)
    padded = jnp.concatenate([node_rows, jnp.zeros((1, row_width), node_rows.dtype)], axis=0)
    sender_rows = jnp.take(table, senders, axis=0)
    receiver_rows = jnp.take(padded, target, axis=0)
    linear = jnp.dot(edge_rows, weight_in[:row_width], preferred_element_type=jnp.float32)
    linear = linear + jnp.dot(sender_rows, weight_in[row_width:2 * row_width], preferred_element_type=jnp.float32)
    linear = linear + jnp.dot(receiver_rows, weight_in[2 * row_width:], preferred_element_type=jnp.float32)
    hidden = jax.nn.silu(linear).astype(jnp.bfloat16)
    normed = layer_norm(jnp.dot(hidden, weight_out, preferred_element_type=jnp.float32))
    new_edges = (edge_rows.astype(jnp.float32) + normed).astype(jnp.bfloat16)
    summed = jax.ops.segment_sum(new_edges.astype(jnp.float32), target, num_segments=node_count + 1)[:node_count]
    return (new_edges, summed)

def node_pass(node_rows, summed, weight_in, weight_out):
    row_width = node_rows.shape[1]
    linear = jnp.dot(node_rows, weight_in[:row_width], preferred_element_type=jnp.float32)
    linear = linear + jnp.dot(summed.astype(jnp.bfloat16), weight_in[row_width:], preferred_element_type=jnp.float32)
    hidden = jax.nn.silu(linear).astype(jnp.bfloat16)
    normed = layer_norm(jnp.dot(hidden, weight_out, preferred_element_type=jnp.float32))
    return (node_rows.astype(jnp.float32) + normed).astype(jnp.bfloat16)

def fine_step(node_rows, edge_rows, senders, receivers, halo_list, weights):
    nodes_split = node_rows.reshape(PARTITIONS, NODE_DEV, LATENT)
    send_lists = halo_list.reshape(PARTITIONS, 5, SLOT)
    outgoing = jax.vmap(lambda block_rows, picked: jnp.take(block_rows, picked, axis=0))(nodes_split, send_lists)
    offsets = (1, -1, 2, -2, PARTITIONS // 2)
    pieces = [jnp.roll(outgoing[:, number], offset, axis=0) for number, offset in enumerate(offsets)]
    tables = jnp.concatenate([nodes_split] + pieces, axis=1)

    def one_partition(packed):
        own_nodes, own_table, own_edges, own_send, own_recv = packed
        new_edges, summed = edge_pass(own_nodes, own_table, own_edges, own_send, own_recv, weights[0], weights[1])
        return (node_pass(own_nodes, summed, weights[2], weights[3]), new_edges)
    new_nodes, new_edges = lax.map(one_partition, (nodes_split, tables, edge_rows.reshape(PARTITIONS, EDGE_DEV, LATENT), senders.reshape(PARTITIONS, EDGE_DEV), receivers.reshape(PARTITIONS, EDGE_DEV)))
    return (new_nodes.reshape(NODES, LATENT), new_edges.reshape(EDGES, LATENT))

def reference(node_latent, edge_latent, coarse_edge_latent, edge_sender, edge_receiver, halo_list, parent, coarse_sender, coarse_receiver, first_edge_in, first_edge_out, first_node_in, first_node_out, coarse_edge_in, coarse_edge_out, coarse_node_in, coarse_node_out, second_edge_in, second_edge_out, second_node_in, second_node_out):
    first_nodes, first_edges = fine_step(node_latent, edge_latent, edge_sender, edge_receiver, halo_list, (first_edge_in, first_edge_out, first_node_in, first_node_out))
    grouped = first_nodes.reshape(BLOCKS, 4 * NODE_DEV, LATENT)
    grouped_parents = parent.reshape(BLOCKS, 4 * NODE_DEV)

    def pool_block(packed):
        block_rows, block_parents = packed
        pooled_sum = jax.ops.segment_sum(block_rows.astype(jnp.float32), block_parents, num_segments=NODE_DEV)
        child_count = jax.ops.segment_sum(jnp.ones(block_parents.shape, jnp.float32), block_parents, num_segments=NODE_DEV)
        return (pooled_sum / child_count[:, None]).astype(jnp.bfloat16)
    coarse_rows = lax.map(pool_block, (grouped, grouped_parents))
    coarse_tables = jnp.concatenate([coarse_rows, jnp.roll(coarse_rows, 1, axis=0), jnp.roll(coarse_rows, -1, axis=0)], axis=1)

    def coarse_block(packed):
        own_rows, own_table, own_edges, own_send, own_recv = packed
        unused_edges, summed = edge_pass(own_rows, own_table, own_edges, own_send, own_recv, coarse_edge_in, coarse_edge_out)
        return node_pass(own_rows, summed, coarse_node_in, coarse_node_out)
    coarse_new = lax.map(coarse_block, (coarse_rows, coarse_tables, coarse_edge_latent.reshape(BLOCKS, 4 * CEDGE_DEV, LATENT), coarse_sender.reshape(BLOCKS, 4 * CEDGE_DEV), coarse_receiver.reshape(BLOCKS, 4 * CEDGE_DEV)))
    lifted = jax.vmap(lambda block_rows, picked: jnp.take(block_rows, picked, axis=0))(coarse_new, grouped_parents)
    middle_nodes = (first_nodes.astype(jnp.float32) + lifted.reshape(NODES, LATENT).astype(jnp.float32)).astype(jnp.bfloat16)
    updated_nodes, second_edges = fine_step(middle_nodes, first_edges, edge_sender, edge_receiver, halo_list, (second_edge_in, second_edge_out, second_node_in, second_node_out))
    return updated_nodes
```

```python
import functools

import jax
import jax.numpy as jnp
from jax import lax
from jax.experimental import pallas as pl
from jax.experimental.pallas import tpu as pltpu
from jax.sharding import PartitionSpec as P

BF = jnp.bfloat16
F32 = jnp.float32
MESH = pl.DeviceIdType.MESH
LANES = 128
GROUP = 4


def round_up(value, unit):
    return -(-value // unit) * unit


def mm(left, right):
    return jnp.dot(left, right, preferred_element_type=F32)


def silu(value):
    half = 0.5 * value
    return half + half * jnp.tanh(half)


def centred_weight(weight):
    wide = weight.astype(F32)
    wide = wide - jnp.mean(wide, axis=-1, keepdims=True)
    high = wide.astype(BF)
    low = (wide - high.astype(F32)).astype(BF)
    return jnp.concatenate([high, low], axis=0)


def normed_product(hidden, weight_pair):
    shifted = mm(jnp.concatenate([hidden, hidden], axis=1), weight_pair)
    width = shifted.shape[1]
    average = jnp.full((width, width), 1.0 / width, BF)
    spread = mm((shifted * shifted).astype(BF), average)
    return shifted * lax.rsqrt(spread + 1e-05)


def spread_column(index_row):
    return jnp.broadcast_to(index_row, (LANES, LANES)).T


def one_hot_columns(index_row, count, first=0):
    column = spread_column(index_row)
    lane = lax.broadcasted_iota(jnp.int32, (LANES, LANES), 1)
    pieces = [
        (column == lane + (first + start)).astype(F32).astype(BF)
        for start in range(0, count, LANES)
    ]
    return jnp.concatenate(pieces, axis=1)


def one_hot_rows(index_row, count, first=0):
    row = lax.broadcasted_iota(jnp.int32, (count, LANES), 0) + first
    return (row == jnp.broadcast_to(index_row, (count, LANES))).astype(F32).astype(BF)


def node_update(nodes, summed, weight_in, weight_pair):
    both = jnp.concatenate([nodes, summed.astype(BF)], axis=1)
    hidden = silu(mm(both, weight_in)).astype(BF)
    return (nodes.astype(F32) + normed_product(hidden, weight_pair)).astype(BF)


def kernel(
    dom,
    slot,
    nodes_ref,
    edges_ref,
    cedges_ref,
    send_ref,
    recv_ref,
    halo_ref,
    parent_ref,
    csend_ref,
    crecv_ref,
    fei_ref,
    feo_ref,
    fni_ref,
    fno_ref,
    cei_ref,
    ceo_ref,
    cni_ref,
    cno_ref,
    sei_ref,
    seo_ref,
    sni_ref,
    sno_ref,
    out_ref,
    hot_s,
    hot_t,
    chot_s,
    chot_t,
    halo_hot,
    parent_hot,
    gathered,
    cgathered,
    new_edges,
    cnew_edges,
    halo_out,
    halo_in,
    parents_in,
    pool_out,
    pool_in,
    ctable,
    agg_out,
    agg_in,
    cnew,
    nodes_mid,
    send_sem,
    halo_sem,
    parent_sem,
    pool_sem,
    table_sem,
    agg_sem,
    cnew_sem,
):
    node_count = nodes_ref.shape[0]
    edge_count = edges_ref.shape[0]
    cedge_count = cedges_ref.shape[0]
    table_rows = hot_s.shape[1] - node_count
    quarter = node_count // GROUP
    me = lax.axis_index("dom")
    rank = lax.rem(me, GROUP)
    base = me - rank
    offsets = (1, -1, 2, -2, dom // 2)

    def away(offset):
        return lax.rem(me + (offset + dom), dom)

    def mate(step):
        return base + lax.rem(rank + step, GROUP)

    barrier = pltpu.get_barrier_semaphore()
    ahead = lax.rem(base + GROUP, dom)
    behind = lax.rem(base + dom - GROUP, dom)
    greeted = [away(offset) for offset in offsets] + [away(-(dom // 2))]
    greeted += [mate(step) for step in range(1, GROUP)]
    greeted += [ahead + step for step in range(GROUP)]
    greeted += [behind + step for step in range(GROUP)]
    for device in greeted:
        pl.semaphore_signal(barrier, inc=1, device_id={"dom": device}, device_id_type=MESH)

    started = []

    def send(source, target, send_at, recv, device):
        copy = pltpu.make_async_remote_copy(
            src_ref=source,
            dst_ref=target,
            send_sem=send_sem.at[send_at],
            recv_sem=recv,
            device_id={"dom": device},
            device_id_type=MESH,
        )
        copy.start()
        started.append(copy)
        return copy

    for block in range(halo_hot.shape[0] // LANES):
        halo_hot[block * LANES : (block + 1) * LANES, :] = one_hot_columns(
            halo_ref[block : block + 1, :], node_count
        )
    halo_out[0] = mm(halo_hot[...], nodes_ref[...]).astype(BF)

    pl.semaphore_wait(barrier, len(greeted))

    def send_halo(turn):
        copies = []
        for number, offset in enumerate(offsets):
            rows = pl.ds(number * slot, slot)
            copies.append(
                send(
                    halo_out.at[turn, rows],
                    halo_in.at[turn, rows],
                    turn * 5 + number,
                    halo_sem.at[turn, number],
                    away(offset),
                )
            )
        return copies

    first_halo = send_halo(0)
    parent_copies = [
        send(parent_ref, parents_in.at[step - 1], 10 + step - 1, parent_sem.at[step - 1], mate(step))
        for step in range(1, GROUP)
    ]

    def fine_hot(block, carry):
        rows = pl.ds(pl.multiple_of(block * LANES, LANES), LANES)
        sender = send_ref[pl.ds(block, 1), :]
        receiver = recv_ref[pl.ds(block, 1), :]
        hot_s[rows, :table_rows] = one_hot_columns(sender, table_rows)
        hot_s[rows, table_rows:] = one_hot_columns(receiver, node_count)
        hot_t[:, rows] = one_hot_rows(receiver, node_count)
        return carry

    def coarse_hot(block, carry):
        rows = pl.ds(pl.multiple_of(block * LANES, LANES), LANES)
        sender = csend_ref[pl.ds(block, 1), :]
        receiver = crecv_ref[pl.ds(block, 1), :]
        chot_s[rows, : 3 * node_count] = one_hot_columns(sender, 3 * node_count)
        chot_s[rows, 3 * node_count :] = one_hot_columns(receiver, node_count)
        chot_t[:, rows] = one_hot_rows(receiver, node_count)
        return carry

    lax.fori_loop(0, edge_count // LANES, fine_hot, 0)

    def edge_loop(source, hot, gathers, weight_in, weight_out, target, count):
        own = weight_in[:LANES, :]
        pair = centred_weight(weight_out[...])
        chunk = 512 if count % 512 == 0 else LANES

        def body(step, carry):
            rows = pl.ds(pl.multiple_of(step * chunk, chunk), chunk)
            old = source[rows, :]
            hidden = silu(mm(old, own) + mm(hot[rows, :], gathers[...])).astype(BF)
            target[rows, :] = (old.astype(F32) + normed_product(hidden, pair)).astype(BF)
            return carry

        lax.fori_loop(0, count // chunk, body, 0)

    def fine_step(turn, nodes, source, halo_copies, wei, weo, wni, wno):
        own = nodes[...]
        gathered[:node_count, :] = mm(own, wei[LANES : 2 * LANES, :]).astype(BF)
        gathered[table_rows:, :] = mm(own, wei[2 * LANES :, :]).astype(BF)
        filled = node_count + 5 * slot
        if filled < table_rows:
            gathered[filled:table_rows, :] = jnp.zeros((table_rows - filled, LANES), BF)
        for copy in halo_copies:
            copy.wait_recv()
        gathered[node_count:filled, :] = mm(
            halo_in[turn], wei[LANES : 2 * LANES, :]
        ).astype(BF)
        edge_loop(source, hot_s, gathered, wei, weo, new_edges, edge_count)
        summed = mm(hot_t[...], new_edges[...])
        return node_update(own, summed, wni[...], centred_weight(wno[...]))

    nodes_one = fine_step(
        0, nodes_ref, edges_ref, first_halo, fei_ref, feo_ref, fni_ref, fno_ref
    )
    nodes_mid[...] = nodes_one

    for block in range(node_count // LANES):
        span = slice(block * LANES, (block + 1) * LANES)
        parent_hot[:, span] = one_hot_rows(parent_ref[block : block + 1, :], node_count)
    pool_out[...] = mm(parent_hot[...], nodes_one).astype(BF)

    def scatter_quarters(outgoing, incoming, send_at, sems):
        copies = []
        for step in range(1, GROUP):
            rows = pl.ds(pl.multiple_of(lax.rem(rank + step, GROUP) * quarter, quarter), quarter)
            copies.append(
                send(outgoing.at[rows], incoming.at[step - 1], send_at + step - 1, sems.at[step - 1], mate(step))
            )
        return copies

    mine = pl.ds(pl.multiple_of(rank * quarter, quarter), quarter)

    def quarter_sum(outgoing, incoming, copies):
        total = outgoing[mine, :].astype(F32)
        for copy in copies:
            copy.wait_recv()
        for step in range(GROUP - 1):
            total = total + incoming[step].astype(F32)
        return total

    pool_copies = scatter_quarters(pool_out, pool_in, 13, pool_sem)
    lax.fori_loop(0, cedge_count // LANES, coarse_hot, 0)
    for copy in parent_copies:
        copy.wait_recv()
    marks = []
    for source in [parent_ref] + [parents_in.at[step] for step in range(GROUP - 1)]:
        marks += [
            one_hot_rows(source[block : block + 1, :], quarter, rank * quarter)
            for block in range(node_count // LANES)
        ]
    marks = jnp.concatenate(marks, axis=1)
    children = mm(marks, jnp.ones((marks.shape[1], LANES), BF))
    pooled = quarter_sum(pool_out, pool_in, pool_copies)
    ctable[mine, :] = (pooled / children).astype(BF)

    def table_send(number, region, device):
        rows = pl.ds(pl.multiple_of(region * node_count + rank * quarter, quarter), quarter)
        return send(ctable.at[mine], ctable.at[rows], 16 + number, table_sem.at[number], device)

    table_copies = []
    for step in range(1, GROUP):
        table_copies.append(table_send(step - 1, 0, mate(step)))
    for step in range(GROUP):
        to = lax.rem(rank + step, GROUP)
        table_copies.append(table_send(3 + step, 1, ahead + to))
        table_copies.append(table_send(7 + step, 2, behind + to))

    for copy in table_copies[: GROUP - 1]:
        copy.wait_recv()
    own_coarse = ctable[:node_count, :]
    sender_weight = cei_ref[LANES : 2 * LANES, :]
    cgathered[:node_count, :] = mm(own_coarse, sender_weight).astype(BF)
    cgathered[3 * node_count :, :] = mm(own_coarse, cei_ref[2 * LANES :, :]).astype(BF)
    for copy in table_copies[GROUP - 1 :]:
        copy.wait_recv()
    cgathered[node_count : 3 * node_count, :] = mm(
        ctable[node_count:, :], sender_weight
    ).astype(BF)
    edge_loop(cedges_ref, chot_s, cgathered, cei_ref, ceo_ref, cnew_edges, cedge_count)
    agg_out[...] = mm(chot_t[...], cnew_edges[...]).astype(BF)
    agg_copies = scatter_quarters(agg_out, agg_in, 27, agg_sem)
    for block in range(node_count // LANES):
        parent_hot[block * LANES : (block + 1) * LANES, :] = one_hot_columns(
            parent_ref[block : block + 1, :], node_count
        )
    coarse_sum = quarter_sum(agg_out, agg_in, agg_copies)
    cnew[mine, :] = node_update(
        ctable[mine, :], coarse_sum, cni_ref[...], centred_weight(cno_ref[...])
    )
    new_copies = [
        send(cnew.at[mine], cnew.at[mine], 30 + step - 1, cnew_sem.at[step - 1], mate(step))
        for step in range(1, GROUP)
    ]
    for copy in new_copies:
        copy.wait_recv()

    lifted = mm(parent_hot[...], cnew[...])
    middle = (nodes_mid[...].astype(F32) + lifted).astype(BF)
    nodes_mid[...] = middle
    halo_out[1] = mm(halo_hot[...], middle).astype(BF)
    second_halo = send_halo(1)
    out_ref[...] = fine_step(
        1, nodes_mid, new_edges, second_halo, sei_ref, seo_ref, sni_ref, sno_ref
    )
    for copy in started:
        copy.wait_send()


def on_device(*arrays):
    (nodes, edges, cedges, senders, receivers, halo, parent, csenders, creceivers) = arrays[:9]
    weights = arrays[9:]
    dom = lax.axis_size("dom")
    node_count, width = nodes.shape
    edge_count = edges.shape[0]
    cedge_count = cedges.shape[0]
    slot = halo.shape[0] // 5
    halo_rows = round_up(halo.shape[0], LANES)
    table_rows = round_up(node_count + 5 * slot, 256)
    quarter = node_count // GROUP
    halo = jnp.pad(halo, (0, halo_rows - halo.shape[0]))
    rows = lambda index: index.reshape(-1, LANES)
    operands = [nodes, edges, cedges] + [
        rows(index) for index in (senders, receivers, halo, parent, csenders, creceivers)
    ]
    operands += list(weights)
    dma = pltpu.SemaphoreType.DMA
    scratch = [
        pltpu.VMEM((edge_count, table_rows + node_count), BF),
        pltpu.VMEM((node_count, edge_count), BF),
        pltpu.VMEM((cedge_count, 4 * node_count), BF),
        pltpu.VMEM((node_count, cedge_count), BF),
        pltpu.VMEM((halo_rows, node_count), BF),
        pltpu.VMEM((node_count, node_count), BF),
        pltpu.VMEM((table_rows + node_count, width), BF),
        pltpu.VMEM((4 * node_count, width), BF),
        pltpu.VMEM((edge_count, width), BF),
        pltpu.VMEM((cedge_count, width), BF),
        pltpu.VMEM((2, halo_rows, width), BF),
        pltpu.VMEM((2, 5 * slot, width), BF),
        pltpu.VMEM((GROUP - 1, node_count // LANES, LANES), jnp.int32),
        pltpu.VMEM((node_count, width), BF),
        pltpu.VMEM((GROUP - 1, quarter, width), BF),
        pltpu.VMEM((3 * node_count, width), BF),
        pltpu.VMEM((node_count, width), BF),
        pltpu.VMEM((GROUP - 1, quarter, width), BF),
        pltpu.VMEM((node_count, width), BF),
        pltpu.VMEM((node_count, width), BF),
        dma((33,)),
        dma((2, 5)),
        dma((GROUP - 1,)),
        dma((GROUP - 1,)),
        dma((11,)),
        dma((GROUP - 1,)),
        dma((GROUP - 1,)),
    ]
    vmem = pl.BlockSpec(memory_space=pltpu.VMEM)
    return pl.pallas_call(
        functools.partial(kernel, dom, slot),
        out_shape=jax.ShapeDtypeStruct((node_count, width), BF),
        in_specs=[vmem] * len(operands),
        out_specs=vmem,
        scratch_shapes=scratch,
        compiler_params=pltpu.CompilerParams(
            collective_id=0, has_side_effects=True, vmem_limit_bytes=48 * 1024 * 1024
        ),
        cost_estimate=pl.CostEstimate(
            flops=2 * 10**10, bytes_accessed=3 * 10**6, transcendentals=2 * 10**6
        ),
        name="multiscale_block",
    )(*operands)


def solution(mesh):
    rows = P(("grp", "dom"), None)
    flat = P(("grp", "dom"))
    placed = (rows,) * 3 + (flat,) * 6 + (P(),) * 12
    return jax.shard_map(
        on_device, mesh=mesh, in_specs=placed, out_specs=rows, check_vma=False
    )
```

```python
import functools

import jax
import jax.numpy as jnp
from jax import lax
from jax.experimental import pallas as pl
from jax.experimental.pallas import tpu as pltpu
from jax.sharding import PartitionSpec as P

BF = jnp.bfloat16
F32 = jnp.float32
MESH = pl.DeviceIdType.MESH
LANES = 128
GROUP = 4
ARGUMENTS = 21
LOAD_ORDER = (0, 5, 6, 3, 4, 1, 9, 10, 11, 12, 7, 8, 2) + tuple(range(13, 21))


def round_up(value, unit):
    return -(-value // unit) * unit


def mm(left, right):
    return jnp.dot(left, right, preferred_element_type=F32)


def silu(value):
    half = 0.5 * value
    return half + half * jnp.tanh(half)


def centred_weight(weight):
    wide = weight.astype(F32)
    wide = wide - jnp.mean(wide, axis=-1, keepdims=True)
    high = wide.astype(BF)
    low = (wide - high.astype(F32)).astype(BF)
    return jnp.concatenate([high, low], axis=0)


def normed_product(hidden, weight_pair):
    shifted = mm(jnp.concatenate([hidden, hidden], axis=1), weight_pair)
    width = shifted.shape[1]
    average = jnp.full((width, width), 1.0 / width, BF)
    spread = mm((shifted * shifted).astype(BF), average)
    return shifted * lax.rsqrt(spread + 1e-05)


def spread_column(index_row):
    return jnp.broadcast_to(index_row, (LANES, LANES)).T


def one_hot_columns(index_row, count, first=0):
    column = spread_column(index_row)
    lane = lax.broadcasted_iota(jnp.int32, (LANES, LANES), 1)
    pieces = [
        (column == lane + (first + start)).astype(F32).astype(BF)
        for start in range(0, count, LANES)
    ]
    return jnp.concatenate(pieces, axis=1)


def one_hot_rows(index_row, count, first=0):
    row = lax.broadcasted_iota(jnp.int32, (count, LANES), 0) + first
    return (row == jnp.broadcast_to(index_row, (count, LANES))).astype(F32).astype(BF)


def node_update(nodes, summed, weight_in, weight_pair):
    both = jnp.concatenate([nodes, summed.astype(BF)], axis=1)
    hidden = silu(mm(both, weight_in)).astype(BF)
    return (nodes.astype(F32) + normed_product(hidden, weight_pair)).astype(BF)


def kernel(
    dom,
    slot,
    *refs,
):
    given = refs[:ARGUMENTS]
    out_ref = refs[ARGUMENTS]
    local = refs[ARGUMENTS + 1 : 2 * ARGUMENTS + 1]
    (
        nodes_ref,
        edges_ref,
        cedges_ref,
        send_ref,
        recv_ref,
        halo_ref,
        parent_ref,
        csend_ref,
        crecv_ref,
        fei_ref,
        feo_ref,
        fni_ref,
        fno_ref,
        cei_ref,
        ceo_ref,
        cni_ref,
        cno_ref,
        sei_ref,
        seo_ref,
        sni_ref,
        sno_ref,
    ) = local
    (
        hot_s,
        hot_t,
        chot_s,
        chot_t,
        halo_hot,
        parent_hot,
        gathered,
        cgathered,
        new_edges,
        cnew_edges,
        halo_out,
        halo_in,
        parents_in,
        pool_out,
        pool_in,
        ctable,
        agg_out,
        agg_in,
        cnew,
        nodes_mid,
        send_sem,
        halo_sem,
        parent_sem,
        pool_sem,
        table_sem,
        agg_sem,
        cnew_sem,
        load_sem,
    ) = refs[2 * ARGUMENTS + 1 :]
    loads = [
        pltpu.make_async_copy(source, target, load_sem.at[number])
        for number, (source, target) in enumerate(zip(given, local))
    ]
    for number in LOAD_ORDER:
        loads[number].start()

    def arrived(numbers):
        for number in numbers:
            loads[number].wait()

    node_count = nodes_ref.shape[0]
    edge_count = edges_ref.shape[0]
    cedge_count = cedges_ref.shape[0]
    table_rows = hot_s.shape[1] - node_count
    quarter = node_count // GROUP
    me = lax.axis_index("dom")
    rank = lax.rem(me, GROUP)
    base = me - rank
    offsets = (1, -1, 2, -2, dom // 2)

    def away(offset):
        return lax.rem(me + (offset + dom), dom)

    def mate(step):
        return base + lax.rem(rank + step, GROUP)

    barrier = pltpu.get_barrier_semaphore()
    ahead = lax.rem(base + GROUP, dom)
    behind = lax.rem(base + dom - GROUP, dom)
    greeted = [away(offset) for offset in offsets] + [away(-(dom // 2))]
    greeted += [mate(step) for step in range(1, GROUP)]
    greeted += [ahead + step for step in range(GROUP)]
    greeted += [behind + step for step in range(GROUP)]
    for device in greeted:
        pl.semaphore_signal(barrier, inc=1, device_id={"dom": device}, device_id_type=MESH)

    started = []

    def send(source, target, send_at, recv, device):
        copy = pltpu.make_async_remote_copy(
            src_ref=source,
            dst_ref=target,
            send_sem=send_sem.at[send_at],
            recv_sem=recv,
            device_id={"dom": device},
            device_id_type=MESH,
        )
        copy.start()
        started.append(copy)
        return copy

    arrived((0, 5, 6))
    for block in range(halo_hot.shape[0] // LANES):
        halo_hot[block * LANES : (block + 1) * LANES, :] = one_hot_columns(
            halo_ref[block : block + 1, :], node_count
        )
    halo_out[0] = mm(halo_hot[...], nodes_ref[...]).astype(BF)

    pl.semaphore_wait(barrier, len(greeted))

    def send_halo(turn):
        copies = []
        for number, offset in enumerate(offsets):
            rows = pl.ds(number * slot, slot)
            copies.append(
                send(
                    halo_out.at[turn, rows],
                    halo_in.at[turn, rows],
                    turn * 5 + number,
                    halo_sem.at[turn, number],
                    away(offset),
                )
            )
        return copies

    first_halo = send_halo(0)
    parent_copies = [
        send(parent_ref, parents_in.at[step - 1], 10 + step - 1, parent_sem.at[step - 1], mate(step))
        for step in range(1, GROUP)
    ]

    def fine_hot(block, carry):
        rows = pl.ds(pl.multiple_of(block * LANES, LANES), LANES)
        sender = send_ref[pl.ds(block, 1), :]
        receiver = recv_ref[pl.ds(block, 1), :]
        hot_s[rows, :table_rows] = one_hot_columns(sender, table_rows)
        hot_s[rows, table_rows:] = one_hot_columns(receiver, node_count)
        hot_t[:, rows] = one_hot_rows(receiver, node_count)
        return carry

    def coarse_hot(block, carry):
        rows = pl.ds(pl.multiple_of(block * LANES, LANES), LANES)
        sender = csend_ref[pl.ds(block, 1), :]
        receiver = crecv_ref[pl.ds(block, 1), :]
        chot_s[rows, : 3 * node_count] = one_hot_columns(sender, 3 * node_count)
        chot_s[rows, 3 * node_count :] = one_hot_columns(receiver, node_count)
        chot_t[:, rows] = one_hot_rows(receiver, node_count)
        return carry

    arrived((3, 4))
    lax.fori_loop(0, edge_count // LANES, fine_hot, 0)
    arrived((1, 2, 7, 8) + tuple(range(9, 21)))

    def edge_loop(source, hot, gathers, weight_in, weight_out, target, count):
        own = weight_in[:LANES, :]
        pair = centred_weight(weight_out[...])
        chunk = 512 if count % 512 == 0 else LANES

        def body(step, carry):
            rows = pl.ds(pl.multiple_of(step * chunk, chunk), chunk)
            old = source[rows, :]
            hidden = silu(mm(old, own) + mm(hot[rows, :], gathers[...])).astype(BF)
            target[rows, :] = (old.astype(F32) + normed_product(hidden, pair)).astype(BF)
            return carry

        lax.fori_loop(0, count // chunk, body, 0)

    def fine_step(turn, nodes, source, halo_copies, wei, weo, wni, wno):
        own = nodes[...]
        gathered[:node_count, :] = mm(own, wei[LANES : 2 * LANES, :]).astype(BF)
        gathered[table_rows:, :] = mm(own, wei[2 * LANES :, :]).astype(BF)
        filled = node_count + 5 * slot
        if filled < table_rows:
            gathered[filled:table_rows, :] = jnp.zeros((table_rows - filled, LANES), BF)
        for copy in halo_copies:
            copy.wait_recv()
        gathered[node_count:filled, :] = mm(
            halo_in[turn], wei[LANES : 2 * LANES, :]
        ).astype(BF)
        edge_loop(source, hot_s, gathered, wei, weo, new_edges, edge_count)
        summed = mm(hot_t[...], new_edges[...])
        return node_update(own, summed, wni[...], centred_weight(wno[...]))

    nodes_one = fine_step(
        0, nodes_ref, edges_ref, first_halo, fei_ref, feo_ref, fni_ref, fno_ref
    )
    nodes_mid[...] = nodes_one

    for block in range(node_count // LANES):
        span = slice(block * LANES, (block + 1) * LANES)
        parent_hot[:, span] = one_hot_rows(parent_ref[block : block + 1, :], node_count)
    pool_out[...] = mm(parent_hot[...], nodes_one).astype(BF)

    def scatter_quarters(outgoing, incoming, send_at, sems):
        copies = []
        for step in range(1, GROUP):
            rows = pl.ds(pl.multiple_of(lax.rem(rank + step, GROUP) * quarter, quarter), quarter)
            copies.append(
                send(outgoing.at[rows], incoming.at[step - 1], send_at + step - 1, sems.at[step - 1], mate(step))
            )
        return copies

    mine = pl.ds(pl.multiple_of(rank * quarter, quarter), quarter)

    def quarter_sum(outgoing, incoming, copies):
        total = outgoing[mine, :].astype(F32)
        for copy in copies:
            copy.wait_recv()
        for step in range(GROUP - 1):
            total = total + incoming[step].astype(F32)
        return total

    pool_copies = scatter_quarters(pool_out, pool_in, 13, pool_sem)
    lax.fori_loop(0, cedge_count // LANES, coarse_hot, 0)
    for copy in parent_copies:
        copy.wait_recv()
    marks = []
    for source in [parent_ref] + [parents_in.at[step] for step in range(GROUP - 1)]:
        marks += [
            one_hot_rows(source[block : block + 1, :], quarter, rank * quarter)
            for block in range(node_count // LANES)
        ]
    marks = jnp.concatenate(marks, axis=1)
    children = mm(marks, jnp.ones((marks.shape[1], LANES), BF))
    pooled = quarter_sum(pool_out, pool_in, pool_copies)
    ctable[mine, :] = (pooled / children).astype(BF)

    def table_send(number, region, device):
        rows = pl.ds(pl.multiple_of(region * node_count + rank * quarter, quarter), quarter)
        return send(ctable.at[mine], ctable.at[rows], 16 + number, table_sem.at[number], device)

    table_copies = []
    for step in range(1, GROUP):
        table_copies.append(table_send(step - 1, 0, mate(step)))
    for step in range(GROUP):
        to = lax.rem(rank + step, GROUP)
        table_copies.append(table_send(3 + step, 1, ahead + to))
        table_copies.append(table_send(7 + step, 2, behind + to))

    for copy in table_copies[: GROUP - 1]:
        copy.wait_recv()
    own_coarse = ctable[:node_count, :]
    sender_weight = cei_ref[LANES : 2 * LANES, :]
    cgathered[:node_count, :] = mm(own_coarse, sender_weight).astype(BF)
    cgathered[3 * node_count :, :] = mm(own_coarse, cei_ref[2 * LANES :, :]).astype(BF)
    for copy in table_copies[GROUP - 1 :]:
        copy.wait_recv()
    cgathered[node_count : 3 * node_count, :] = mm(
        ctable[node_count:, :], sender_weight
    ).astype(BF)
    edge_loop(cedges_ref, chot_s, cgathered, cei_ref, ceo_ref, cnew_edges, cedge_count)
    agg_out[...] = mm(chot_t[...], cnew_edges[...]).astype(BF)
    agg_copies = scatter_quarters(agg_out, agg_in, 27, agg_sem)
    for block in range(node_count // LANES):
        parent_hot[block * LANES : (block + 1) * LANES, :] = one_hot_columns(
            parent_ref[block : block + 1, :], node_count
        )
    coarse_sum = quarter_sum(agg_out, agg_in, agg_copies)
    cnew[mine, :] = node_update(
        ctable[mine, :], coarse_sum, cni_ref[...], centred_weight(cno_ref[...])
    )
    new_copies = [
        send(cnew.at[mine], cnew.at[mine], 30 + step - 1, cnew_sem.at[step - 1], mate(step))
        for step in range(1, GROUP)
    ]
    for copy in new_copies:
        copy.wait_recv()

    lifted = mm(parent_hot[...], cnew[...])
    middle = (nodes_mid[...].astype(F32) + lifted).astype(BF)
    nodes_mid[...] = middle
    halo_out[1] = mm(halo_hot[...], middle).astype(BF)
    second_halo = send_halo(1)
    out_ref[...] = fine_step(
        1, nodes_mid, new_edges, second_halo, sei_ref, seo_ref, sni_ref, sno_ref
    )
    for copy in started:
        copy.wait_send()


def on_device(*arrays):
    (nodes, edges, cedges, senders, receivers, halo, parent, csenders, creceivers) = arrays[:9]
    weights = arrays[9:]
    dom = lax.axis_size("dom")
    node_count, width = nodes.shape
    edge_count = edges.shape[0]
    cedge_count = cedges.shape[0]
    slot = halo.shape[0] // 5
    halo_rows = round_up(halo.shape[0], LANES)
    table_rows = round_up(node_count + 5 * slot, 256)
    quarter = node_count // GROUP
    halo = jnp.pad(halo, (0, halo_rows - halo.shape[0]))
    rows = lambda index: index.reshape(-1, LANES)
    operands = [nodes, edges, cedges] + [
        rows(index) for index in (senders, receivers, halo, parent, csenders, creceivers)
    ]
    operands += list(weights)
    dma = pltpu.SemaphoreType.DMA
    scratch = [pltpu.VMEM(operand.shape, operand.dtype) for operand in operands]
    scratch += [
        pltpu.VMEM((edge_count, table_rows + node_count), BF),
        pltpu.VMEM((node_count, edge_count), BF),
        pltpu.VMEM((cedge_count, 4 * node_count), BF),
        pltpu.VMEM((node_count, cedge_count), BF),
        pltpu.VMEM((halo_rows, node_count), BF),
        pltpu.VMEM((node_count, node_count), BF),
        pltpu.VMEM((table_rows + node_count, width), BF),
        pltpu.VMEM((4 * node_count, width), BF),
        pltpu.VMEM((edge_count, width), BF),
        pltpu.VMEM((cedge_count, width), BF),
        pltpu.VMEM((2, halo_rows, width), BF),
        pltpu.VMEM((2, 5 * slot, width), BF),
        pltpu.VMEM((GROUP - 1, node_count // LANES, LANES), jnp.int32),
        pltpu.VMEM((node_count, width), BF),
        pltpu.VMEM((GROUP - 1, quarter, width), BF),
        pltpu.VMEM((3 * node_count, width), BF),
        pltpu.VMEM((node_count, width), BF),
        pltpu.VMEM((GROUP - 1, quarter, width), BF),
        pltpu.VMEM((node_count, width), BF),
        pltpu.VMEM((node_count, width), BF),
        dma((33,)),
        dma((2, 5)),
        dma((GROUP - 1,)),
        dma((GROUP - 1,)),
        dma((11,)),
        dma((GROUP - 1,)),
        dma((GROUP - 1,)),
        dma((ARGUMENTS,)),
    ]
    vmem = pl.BlockSpec(memory_space=pltpu.VMEM)
    return pl.pallas_call(
        functools.partial(kernel, dom, slot),
        out_shape=jax.ShapeDtypeStruct((node_count, width), BF),
        in_specs=[pl.BlockSpec(memory_space=pltpu.HBM)] * len(operands),
        out_specs=vmem,
        scratch_shapes=scratch,
        compiler_params=pltpu.CompilerParams(
            collective_id=0, has_side_effects=True, vmem_limit_bytes=60 * 1024 * 1024
        ),
        cost_estimate=pl.CostEstimate(
            flops=2 * 10**10, bytes_accessed=3 * 10**6, transcendentals=2 * 10**6
        ),
        name="multiscale_block",
    )(*operands)


def solution(mesh):
    rows = P(("grp", "dom"), None)
    flat = P(("grp", "dom"))
    placed = (rows,) * 3 + (flat,) * 6 + (P(),) * 12
    return jax.shard_map(
        on_device, mesh=mesh, in_specs=placed, out_specs=rows, check_vma=False
    )
```

```python
import functools

import jax
import jax.numpy as jnp
from jax import lax
from jax.experimental import pallas as pl
from jax.experimental.pallas import tpu as pltpu
from jax.sharding import PartitionSpec as P

BF = jnp.bfloat16
F32 = jnp.float32
MESH = pl.DeviceIdType.MESH
LANES = 128
GROUP = 4
ARGUMENTS = 21
LOAD_ORDER = (0, 5, 6, 3, 4, 1, 9, 10, 11, 12, 7, 8, 2) + tuple(range(13, 21))


def round_up(value, unit):
    return -(-value // unit) * unit


def mm(left, right):
    return jnp.dot(left, right, preferred_element_type=F32)


def silu(value):
    half = 0.5 * value
    return half + half * jnp.tanh(half)


def centred_weight(weight):
    wide = weight.astype(F32)
    wide = wide - jnp.mean(wide, axis=-1, keepdims=True)
    high = wide.astype(BF)
    low = (wide - high.astype(F32)).astype(BF)
    return jnp.concatenate([high, low], axis=0)


def normed_product(hidden, weight_pair):
    shifted = mm(jnp.concatenate([hidden, hidden], axis=1), weight_pair)
    width = shifted.shape[1]
    average = jnp.full((width, width), 1.0 / width, BF)
    spread = mm((shifted * shifted).astype(BF), average)
    return shifted * lax.rsqrt(spread + 1e-05)


def spread_column(index_row):
    return jnp.broadcast_to(index_row, (LANES, LANES)).T


def one_hot_columns(index_row, count, first=0):
    column = spread_column(index_row)
    lane = lax.broadcasted_iota(jnp.int32, (LANES, LANES), 1)
    pieces = [
        (column == lane + (first + start)).astype(F32).astype(BF)
        for start in range(0, count, LANES)
    ]
    return jnp.concatenate(pieces, axis=1)


def one_hot_rows(index_row, count, first=0):
    row = lax.broadcasted_iota(jnp.int32, (count, LANES), 0) + first
    return (row == jnp.broadcast_to(index_row, (count, LANES))).astype(F32).astype(BF)


def node_update(nodes, summed, weight_in, weight_pair):
    both = jnp.concatenate([nodes, summed.astype(BF)], axis=1)
    hidden = silu(mm(both, weight_in)).astype(BF)
    return (nodes.astype(F32) + normed_product(hidden, weight_pair)).astype(BF)


def kernel(
    dom,
    slot,
    *refs,
):
    given = refs[:ARGUMENTS]
    out_ref = refs[ARGUMENTS]
    local = refs[ARGUMENTS + 1 : 2 * ARGUMENTS + 1]
    (
        nodes_ref,
        edges_ref,
        cedges_ref,
        send_ref,
        recv_ref,
        halo_ref,
        parent_ref,
        csend_ref,
        crecv_ref,
        fei_ref,
        feo_ref,
        fni_ref,
        fno_ref,
        cei_ref,
        ceo_ref,
        cni_ref,
        cno_ref,
        sei_ref,
        seo_ref,
        sni_ref,
        sno_ref,
    ) = local
    (
        hot_s,
        hot_t,
        chot_s,
        chot_t,
        halo_hot,
        parent_hot,
        gathered,
        cgathered,
        new_edges,
        cnew_edges,
        halo_out,
        halo_in,
        parents_in,
        pool_out,
        pool_in,
        ctable,
        agg_out,
        agg_in,
        cnew,
        nodes_mid,
        send_sem,
        halo_sem,
        parent_sem,
        pool_sem,
        table_sem,
        agg_sem,
        cnew_sem,
        load_sem,
    ) = refs[2 * ARGUMENTS + 1 :]
    loads = [
        pltpu.make_async_copy(source, target, load_sem.at[number])
        for number, (source, target) in enumerate(zip(given, local))
    ]
    for number in LOAD_ORDER:
        loads[number].start()

    def arrived(numbers):
        for number in numbers:
            loads[number].wait()

    node_count = nodes_ref.shape[0]
    edge_count = edges_ref.shape[0]
    cedge_count = cedges_ref.shape[0]
    table_rows = hot_s.shape[1] - node_count
    quarter = node_count // GROUP
    me = lax.axis_index("dom")
    rank = lax.rem(me, GROUP)
    base = me - rank
    offsets = (1, -1, 2, -2, dom // 2)

    def away(offset):
        return lax.rem(me + (offset + dom), dom)

    def mate(step):
        return base + lax.rem(rank + step, GROUP)

    barrier = pltpu.get_barrier_semaphore()
    ahead = lax.rem(base + GROUP, dom)
    behind = lax.rem(base + dom - GROUP, dom)
    greeted = [away(offset) for offset in offsets] + [away(-(dom // 2))]
    greeted += [mate(step) for step in range(1, GROUP)]
    greeted += [ahead + step for step in range(GROUP)]
    greeted += [behind + step for step in range(GROUP)]
    for device in greeted:
        pl.semaphore_signal(barrier, inc=1, device_id={"dom": device}, device_id_type=MESH)

    started = []

    def send(source, target, send_at, recv, device):
        copy = pltpu.make_async_remote_copy(
            src_ref=source,
            dst_ref=target,
            send_sem=send_sem.at[send_at],
            recv_sem=recv,
            device_id={"dom": device},
            device_id_type=MESH,
        )
        copy.start()
        started.append(copy)
        return copy

    arrived((0, 5, 6))
    for block in range(halo_hot.shape[0] // LANES):
        halo_hot[block * LANES : (block + 1) * LANES, :] = one_hot_columns(
            halo_ref[block : block + 1, :], node_count
        )
    halo_out[0] = mm(halo_hot[...], nodes_ref[...]).astype(BF)

    pl.semaphore_wait(barrier, len(greeted))

    def send_halo(turn):
        copies = []
        for number, offset in enumerate(offsets):
            rows = pl.ds(number * slot, slot)
            copies.append(
                send(
                    halo_out.at[turn, rows],
                    halo_in.at[turn, rows],
                    turn * 5 + number,
                    halo_sem.at[turn, number],
                    away(offset),
                )
            )
        return copies

    first_halo = send_halo(0)
    parent_copies = [
        send(parent_ref, parents_in.at[step - 1], 10 + step - 1, parent_sem.at[step - 1], mate(step))
        for step in range(1, GROUP)
    ]

    def fine_hot(block, carry):
        rows = pl.ds(pl.multiple_of(block * LANES, LANES), LANES)
        sender = send_ref[pl.ds(block, 1), :]
        receiver = recv_ref[pl.ds(block, 1), :]
        hot_s[rows, :table_rows] = one_hot_columns(sender, table_rows)
        hot_s[rows, table_rows:] = one_hot_columns(receiver, node_count)
        hot_t[:, rows] = one_hot_rows(receiver, node_count)
        return carry

    def coarse_hot(block, carry):
        rows = pl.ds(pl.multiple_of(block * LANES, LANES), LANES)
        sender = csend_ref[pl.ds(block, 1), :]
        receiver = crecv_ref[pl.ds(block, 1), :]
        chot_s[rows, : 3 * node_count] = one_hot_columns(sender, 3 * node_count)
        chot_s[rows, 3 * node_count :] = one_hot_columns(receiver, node_count)
        chot_t[:, rows] = one_hot_rows(receiver, node_count)
        return carry

    arrived((3, 4))
    lax.fori_loop(0, edge_count // LANES, fine_hot, 0)
    arrived((1, 2, 7, 8) + tuple(range(9, 21)))

    def edge_loop(source, hot, gathers, weight_in, weight_out, target, count):
        own = weight_in[:LANES, :]
        pair = centred_weight(weight_out[...])
        chunk = 512 if count % 512 == 0 else LANES

        def body(step, carry):
            rows = pl.ds(pl.multiple_of(step * chunk, chunk), chunk)
            old = source[rows, :]
            hidden = silu(mm(old, own) + mm(hot[rows, :], gathers[...])).astype(BF)
            target[rows, :] = (old.astype(F32) + normed_product(hidden, pair)).astype(BF)
            return carry

        lax.fori_loop(0, count // chunk, body, 0)

    def fine_step(turn, nodes, source, halo_copies, wei, weo, wni, wno):
        own = nodes[...]
        gathered[:node_count, :] = mm(own, wei[LANES : 2 * LANES, :]).astype(BF)
        gathered[table_rows:, :] = mm(own, wei[2 * LANES :, :]).astype(BF)
        filled = node_count + 5 * slot
        if filled < table_rows:
            gathered[filled:table_rows, :] = jnp.zeros((table_rows - filled, LANES), BF)
        for copy in halo_copies:
            copy.wait_recv()
        gathered[node_count:filled, :] = mm(
            halo_in[turn], wei[LANES : 2 * LANES, :]
        ).astype(BF)
        edge_loop(source, hot_s, gathered, wei, weo, new_edges, edge_count)
        summed = mm(hot_t[...], new_edges[...])
        return node_update(own, summed, wni[...], centred_weight(wno[...]))

    nodes_one = fine_step(
        0, nodes_ref, edges_ref, first_halo, fei_ref, feo_ref, fni_ref, fno_ref
    )
    nodes_mid[...] = nodes_one

    for block in range(node_count // LANES):
        span = slice(block * LANES, (block + 1) * LANES)
        parent_hot[:, span] = one_hot_rows(parent_ref[block : block + 1, :], node_count)
    pool_out[...] = mm(parent_hot[...], nodes_one).astype(BF)

    def scatter_quarters(outgoing, incoming, send_at, sems):
        copies = []
        for step in range(1, GROUP):
            rows = pl.ds(pl.multiple_of(lax.rem(rank + step, GROUP) * quarter, quarter), quarter)
            copies.append(
                send(outgoing.at[rows], incoming.at[step - 1], send_at + step - 1, sems.at[step - 1], mate(step))
            )
        return copies

    mine = pl.ds(pl.multiple_of(rank * quarter, quarter), quarter)

    def quarter_sum(outgoing, incoming, copies):
        total = outgoing[mine, :].astype(F32)
        for copy in copies:
            copy.wait_recv()
        for step in range(GROUP - 1):
            total = total + incoming[step].astype(F32)
        return total

    pool_copies = scatter_quarters(pool_out, pool_in, 13, pool_sem)
    lax.fori_loop(0, cedge_count // LANES, coarse_hot, 0)
    for copy in parent_copies:
        copy.wait_recv()
    marks = []
    for source in [parent_ref] + [parents_in.at[step] for step in range(GROUP - 1)]:
        marks += [
            one_hot_rows(source[block : block + 1, :], quarter, rank * quarter)
            for block in range(node_count // LANES)
        ]
    marks = jnp.concatenate(marks, axis=1)
    children = mm(marks, jnp.ones((marks.shape[1], LANES), BF))
    pooled = quarter_sum(pool_out, pool_in, pool_copies)
    ctable[mine, :] = (pooled / children).astype(BF)

    def table_send(number, region, device):
        rows = pl.ds(pl.multiple_of(region * node_count + rank * quarter, quarter), quarter)
        return send(ctable.at[mine], ctable.at[rows], 16 + number, table_sem.at[number], device)

    table_copies = []
    for step in range(1, GROUP):
        table_copies.append(table_send(step - 1, 0, mate(step)))
    far_copies = [table_send(3, 1, ahead + rank), table_send(4, 2, behind + rank)]
    for region, far in enumerate(far_copies, 1):
        far.wait_recv()
        rows = pl.ds(pl.multiple_of(region * node_count + rank * quarter, quarter), quarter)
        for step in range(1, GROUP):
            number = 1 + 3 * region + step
            table_copies.append(
                send(ctable.at[rows], ctable.at[rows], 16 + number, table_sem.at[number], mate(step))
            )

    for copy in table_copies[: GROUP - 1]:
        copy.wait_recv()
    own_coarse = ctable[:node_count, :]
    sender_weight = cei_ref[LANES : 2 * LANES, :]
    cgathered[:node_count, :] = mm(own_coarse, sender_weight).astype(BF)
    cgathered[3 * node_count :, :] = mm(own_coarse, cei_ref[2 * LANES :, :]).astype(BF)
    for copy in table_copies[GROUP - 1 :]:
        copy.wait_recv()
    cgathered[node_count : 3 * node_count, :] = mm(
        ctable[node_count:, :], sender_weight
    ).astype(BF)
    edge_loop(cedges_ref, chot_s, cgathered, cei_ref, ceo_ref, cnew_edges, cedge_count)
    agg_out[...] = mm(chot_t[...], cnew_edges[...]).astype(BF)
    agg_copies = scatter_quarters(agg_out, agg_in, 27, agg_sem)
    for block in range(node_count // LANES):
        parent_hot[block * LANES : (block + 1) * LANES, :] = one_hot_columns(
            parent_ref[block : block + 1, :], node_count
        )
    coarse_sum = quarter_sum(agg_out, agg_in, agg_copies)
    cnew[mine, :] = node_update(
        ctable[mine, :], coarse_sum, cni_ref[...], centred_weight(cno_ref[...])
    )
    new_copies = [
        send(cnew.at[mine], cnew.at[mine], 30 + step - 1, cnew_sem.at[step - 1], mate(step))
        for step in range(1, GROUP)
    ]
    for copy in new_copies:
        copy.wait_recv()

    lifted = mm(parent_hot[...], cnew[...])
    middle = (nodes_mid[...].astype(F32) + lifted).astype(BF)
    nodes_mid[...] = middle
    halo_out[1] = mm(halo_hot[...], middle).astype(BF)
    second_halo = send_halo(1)
    out_ref[...] = fine_step(
        1, nodes_mid, new_edges, second_halo, sei_ref, seo_ref, sni_ref, sno_ref
    )
    for copy in started:
        copy.wait_send()


def on_device(*arrays):
    (nodes, edges, cedges, senders, receivers, halo, parent, csenders, creceivers) = arrays[:9]
    weights = arrays[9:]
    dom = lax.axis_size("dom")
    node_count, width = nodes.shape
    edge_count = edges.shape[0]
    cedge_count = cedges.shape[0]
    slot = halo.shape[0] // 5
    halo_rows = round_up(halo.shape[0], LANES)
    table_rows = round_up(node_count + 5 * slot, 256)
    quarter = node_count // GROUP
    halo = jnp.pad(halo, (0, halo_rows - halo.shape[0]))
    rows = lambda index: index.reshape(-1, LANES)
    operands = [nodes, edges, cedges] + [
        rows(index) for index in (senders, receivers, halo, parent, csenders, creceivers)
    ]
    operands += list(weights)
    dma = pltpu.SemaphoreType.DMA
    scratch = [pltpu.VMEM(operand.shape, operand.dtype) for operand in operands]
    scratch += [
        pltpu.VMEM((edge_count, table_rows + node_count), BF),
        pltpu.VMEM((node_count, edge_count), BF),
        pltpu.VMEM((cedge_count, 4 * node_count), BF),
        pltpu.VMEM((node_count, cedge_count), BF),
        pltpu.VMEM((halo_rows, node_count), BF),
        pltpu.VMEM((node_count, node_count), BF),
        pltpu.VMEM((table_rows + node_count, width), BF),
        pltpu.VMEM((4 * node_count, width), BF),
        pltpu.VMEM((edge_count, width), BF),
        pltpu.VMEM((cedge_count, width), BF),
        pltpu.VMEM((2, halo_rows, width), BF),
        pltpu.VMEM((2, 5 * slot, width), BF),
        pltpu.VMEM((GROUP - 1, node_count // LANES, LANES), jnp.int32),
        pltpu.VMEM((node_count, width), BF),
        pltpu.VMEM((GROUP - 1, quarter, width), BF),
        pltpu.VMEM((3 * node_count, width), BF),
        pltpu.VMEM((node_count, width), BF),
        pltpu.VMEM((GROUP - 1, quarter, width), BF),
        pltpu.VMEM((node_count, width), BF),
        pltpu.VMEM((node_count, width), BF),
        dma((33,)),
        dma((2, 5)),
        dma((GROUP - 1,)),
        dma((GROUP - 1,)),
        dma((11,)),
        dma((GROUP - 1,)),
        dma((GROUP - 1,)),
        dma((ARGUMENTS,)),
    ]
    vmem = pl.BlockSpec(memory_space=pltpu.VMEM)
    return pl.pallas_call(
        functools.partial(kernel, dom, slot),
        out_shape=jax.ShapeDtypeStruct((node_count, width), BF),
        in_specs=[pl.BlockSpec(memory_space=pltpu.HBM)] * len(operands),
        out_specs=vmem,
        scratch_shapes=scratch,
        compiler_params=pltpu.CompilerParams(
            collective_id=0, has_side_effects=True, vmem_limit_bytes=60 * 1024 * 1024
        ),
        cost_estimate=pl.CostEstimate(
            flops=2 * 10**10, bytes_accessed=3 * 10**6, transcendentals=2 * 10**6
        ),
        name="multiscale_block",
    )(*operands)


def solution(mesh):
    rows = P(("grp", "dom"), None)
    flat = P(("grp", "dom"))
    placed = (rows,) * 3 + (flat,) * 6 + (P(),) * 12
    return jax.shard_map(
        on_device, mesh=mesh, in_specs=placed, out_specs=rows, check_vma=False
    )
```
